512 devices in a mesh: dp: 32 (over x, z_lo, core), seq: 16 (over y, z_hi).
Axes of the slice: x: 4, y: 4, z: 16 (z_hi: 4, z_lo: 4; z = z_hi * 4 + z_lo), core: 2. Of those that a mesh axis runs over, the one named last changes fastest.
Arguments:
- query: bfloat16 [32, 2048, 2048], P('dp', 'seq'), may hold values from -6 to 6
- key: bfloat16 [32, 2048, 2048], P('dp', 'seq'), may hold values from -6 to 6
- value: bfloat16 [32, 2048, 2048], P('dp', 'seq'), may hold values from -6 to 6
- patch_map: int32 [32, 2048], P('dp', 'seq'), may hold values from 0 to 127, as said below
- teacher: bfloat16 [32, 128, 1408], P('dp', 'seq'), may hold values from -6 to 6
- proj_in: bfloat16 [2048, 2048], P(None, 'seq'), may hold values from -0.13258252 to 0.13258252
- proj_out: bfloat16 [2048, 1408], P('seq'), may hold values from -0.13258252 to 0.13258252
Outputs:
- grad_query: bfloat16 [32, 2048, 2048], P('dp', 'seq')
- grad_value: bfloat16 [32, 2048, 2048], P('dp', 'seq')
- grad_in: float32 [2048, 2048], P(None, 'seq')
- grad_out: float32 [2048, 1408], P('seq')
The draws below stay inside these ranges and needn't reach their ends.
Inputs may be any that keep to these rules, and one draw needn't show every extreme that they name: `patch_map`: each teacher patch of a clip is named by exactly 16 of that clip's tokens.
All inputs are finite; a program needn't handle non-finite values.
Results may differ from the reference program's by a relative error of at most 0.02.
Values may be sent and summed in bfloat16 or wider, within the bound.
No kernel may reach another device: no remote copies, remote signals or barrier semaphores. Data moves between devices by JAX's collectives and lax.ppermute only.
A program may use at most 64 MiB of HBM per device.

```python
import jax
import jax.numpy as jnp
from jax import lax

HEAD_DIM = 64
HEADS = 32
WIDTH = 2048
HID = 2048
TEACH = 1408
SEQ_LEN = 2048
PATCHES = 128
GROUP = 16
CLIPS = 32


def normal_field(key, shape, scale, bound):
    return jnp.clip(jax.random.normal(key, shape, jnp.float32) * scale, -bound, bound)


def draw_query(key, part):
    key = jax.random.fold_in(key, 1)
    sampled = normal_field(key, (CLIPS, SEQ_LEN, WIDTH), 2.0, 6.0)
    return sampled.astype(jnp.bfloat16)


def draw_key(key, part):
    key = jax.random.fold_in(key, 2)
    sampled = normal_field(key, (CLIPS, SEQ_LEN, WIDTH), 2.0, 6.0)
    return sampled.astype(jnp.bfloat16)


def draw_value(key, part):
    key = jax.random.fold_in(key, 4)
    sampled = normal_field(key, (CLIPS, SEQ_LEN, WIDTH), 1.0, 6.0)
    return sampled.astype(jnp.bfloat16)


def draw_proj_in(key, part):
    key = jax.random.fold_in(key, 5)
    spread = WIDTH ** (-0.5)
    sampled = normal_field(key, (WIDTH, HID), spread, 6.0 * spread)
    return sampled.astype(jnp.bfloat16)


def draw_proj_out(key, part):
    key = jax.random.fold_in(key, 6)
    spread = HID ** (-0.5)
    sampled = normal_field(key, (HID, TEACH), spread, 6.0 * spread)
    return sampled.astype(jnp.bfloat16)


def draw_patch_map(key, part):
    key = jax.random.fold_in(key, 3)
    clip_range = jnp.arange(CLIPS)
    orders = jax.vmap(lambda clip: jax.random.permutation(jax.random.fold_in(key, clip), SEQ_LEN))(clip_range)
    labels = jnp.broadcast_to((jnp.arange(SEQ_LEN, dtype=jnp.int32) // GROUP)[None, :], (CLIPS, SEQ_LEN))
    result = jnp.zeros((CLIPS, SEQ_LEN), jnp.int32)
    return result.at[clip_range[:, None], orders].set(labels)


def drawn_rows(queries, key_rows, values, patch_ids, weight_in, weight_out):
    patch_range = jnp.arange(PATCHES, dtype=jnp.int32)
    highest = lax.Precision.HIGHEST

    def per_head(inputs):
        head_query, head_keys, head_values = inputs
        scores = jnp.dot(head_query, head_keys.T, precision=highest) * 0.125
        weights = jax.nn.softmax(scores, axis=-1)
        return jnp.dot(weights, head_values, precision=highest)

    def per_clip(inputs):
        clip_query, clip_keys, clip_values, clip_ids = inputs
        split = lambda matrix: matrix.reshape(SEQ_LEN, HEADS, HEAD_DIM).transpose(1, 0, 2)
        attended = lax.map(per_head, (split(clip_query), split(clip_keys), split(clip_values)))
        attended = attended.transpose(1, 0, 2).reshape(SEQ_LEN, WIDTH)
        selector = (clip_ids[None, :] == patch_range[:, None]).astype(jnp.float32)
        pooled = jnp.dot(selector, attended, precision=highest) / GROUP
        hidden = jax.nn.silu(jnp.dot(pooled, weight_in, precision=highest))
        projected = jnp.dot(hidden, weight_out, precision=highest)
        return projected * lax.rsqrt(jnp.mean(projected * projected, axis=-1, keepdims=True) + 1e-06)
    return lax.map(per_clip, (queries, key_rows, values, patch_ids))


def draw_teacher(key, part):
    queries = draw_query(key, part)
    key_rows = draw_key(key, part)
    values = draw_value(key, part)
    patch_ids = draw_patch_map(key, part)
    weight_in = draw_proj_in(key, part)
    weight_out = draw_proj_out(key, part)
    key = jax.random.fold_in(key, 7)
    aligned = drawn_rows(queries, key_rows, values, patch_ids, weight_in, weight_out)
    blended = 0.6 * aligned + 0.8 * normal_field(key, (CLIPS, PATCHES, TEACH), 1.0, 6.0)
    return jnp.clip(blended, -6.0, 6.0).astype(jnp.bfloat16)


def setup_inputs(seed: int = 0) -> dict:
    arg_keys = jax.random.split(jax.random.key(seed), 8)
    query = draw_query(jax.random.fold_in(arg_keys[7], 71), 0)
    key = draw_key(jax.random.fold_in(arg_keys[7], 71), 0)
    value = draw_value(jax.random.fold_in(arg_keys[7], 71), 0)
    patch_map = draw_patch_map(jax.random.fold_in(arg_keys[7], 71), 0)
    teacher = draw_teacher(jax.random.fold_in(arg_keys[7], 71), 0)
    proj_in = draw_proj_in(jax.random.fold_in(arg_keys[7], 71), 0)
    proj_out = draw_proj_out(jax.random.fold_in(arg_keys[7], 71), 0)
    return {"query": query, "key": key, "value": value, "patch_map": patch_map, "teacher": teacher, "proj_in": proj_in, "proj_out": proj_out}


SCALE = 0.125
EPSILON = 1e-06

def head_probs(queries, keys):
    scores = jnp.dot(queries, keys.T, preferred_element_type=jnp.float32) * SCALE
    highest = lax.optimization_barrier(jnp.max(scores, axis=-1, keepdims=True))
    weights = jnp.exp(scores - highest)
    return (weights / lax.optimization_barrier(jnp.sum(weights, axis=-1, keepdims=True))).astype(jnp.bfloat16)

def forward_head(inputs):
    queries, keys, values = inputs
    weights = head_probs(queries, keys)
    return jnp.dot(weights, values, preferred_element_type=jnp.float32).astype(jnp.bfloat16)

def backward_head(inputs):
    queries, keys, values, upstream = inputs
    weights = head_probs(queries, keys)
    grad_values = jnp.dot(weights.T, upstream, preferred_element_type=jnp.float32).astype(jnp.bfloat16)
    dprob = jnp.dot(upstream, values.T, preferred_element_type=jnp.float32)
    weights_f = weights.astype(jnp.float32)
    delta = lax.optimization_barrier(jnp.sum(weights_f * dprob, axis=-1, keepdims=True))
    dscore = (weights_f * (dprob - delta) * SCALE).astype(jnp.bfloat16)
    grad_queries = jnp.dot(dscore, keys, preferred_element_type=jnp.float32).astype(jnp.bfloat16)
    return (grad_queries, grad_values)

def split_heads(matrix):
    return matrix.reshape(SEQ_LEN, HEADS, HEAD_DIM).transpose(1, 0, 2)

def join_heads(stacked):
    return stacked.transpose(1, 0, 2).reshape(SEQ_LEN, WIDTH)

def reference(query, key, value, patch_map, teacher, proj_in, proj_out):
    patch_range = jnp.arange(PATCHES, dtype=jnp.int32)

    def per_clip(carried, inputs):
        queries, keys, values, ids, features = inputs
        query_heads = split_heads(queries)
        key_heads = split_heads(keys)
        value_heads = split_heads(values)
        attended = join_heads(lax.map(forward_head, (query_heads, key_heads, value_heads)))
        selector = (ids[None, :] == patch_range[:, None]).astype(jnp.bfloat16)
        pooled = (jnp.dot(selector, attended, preferred_element_type=jnp.float32) / GROUP).astype(jnp.bfloat16)
        preact = jnp.dot(pooled, proj_in, preferred_element_type=jnp.float32)
        hidden = jax.nn.silu(preact).astype(jnp.bfloat16)
        proj = jnp.dot(hidden, proj_out, preferred_element_type=jnp.float32)
        target = features.astype(jnp.float32)
        cross_term = lax.optimization_barrier(jnp.mean(proj * target, axis=-1, keepdims=True))
        proj_power = lax.optimization_barrier(jnp.mean(proj * proj, axis=-1, keepdims=True)) + EPSILON
        teach_power = lax.optimization_barrier(jnp.mean(target * target, axis=-1, keepdims=True)) + EPSILON
        grad_proj = (-(target - cross_term / proj_power * proj) / jnp.sqrt(proj_power * teach_power)).astype(jnp.bfloat16)
        grad_out_clip = jnp.dot(hidden.T, grad_proj, preferred_element_type=jnp.float32)
        grad_hidden = jnp.dot(grad_proj, proj_out.T, preferred_element_type=jnp.float32)
        sigma = jax.nn.sigmoid(preact)
        grad_pre = (grad_hidden * sigma * (1.0 + preact * (1.0 - sigma))).astype(jnp.bfloat16)
        grad_in_clip = jnp.dot(pooled.T, grad_pre, preferred_element_type=jnp.float32)
        grad_pooled = jnp.dot(grad_pre, proj_in.T, preferred_element_type=jnp.float32).astype(jnp.bfloat16)
        grad_attended = (jnp.dot(selector.T, grad_pooled, preferred_element_type=jnp.float32) / GROUP).astype(jnp.bfloat16)
        grad_queries, grad_values = lax.map(backward_head, (query_heads, key_heads, value_heads, split_heads(grad_attended)))
        summed = (carried[0] + grad_in_clip, carried[1] + grad_out_clip)
        return (summed, (join_heads(grad_queries), join_heads(grad_values)))
    start = (jnp.zeros((WIDTH, HID), jnp.float32), jnp.zeros((HID, TEACH), jnp.float32))
    totals, stacked = lax.scan(per_clip, start, (query, key, value, patch_map, teacher))
    return (stacked[0], stacked[1], totals[0], totals[1])
```

```python
import functools

import jax
import jax.numpy as jnp
from jax import lax
from jax.experimental import pallas as pl
from jax.experimental.pallas import tpu as pltpu
from jax.sharding import PartitionSpec as P

BF = jnp.bfloat16
F32 = jnp.float32
NS = 16
NY = 4
NZ = 4
TOK = 128
LEN = 2048
FEAT = 128
PATCHES = 128
PY = 32
TEACH = 1408
WIDTH = 2048
GROUP = 16
EPSILON = 1e-06
ROWS = 3 * TOK + 16
BLK = 256
VMEM = 50 * 1024 * 1024

Y_GROUPS = [[y * 4 + z for y in range(4)] for z in range(4)]
Z_GROUPS = [[y * 4 + z for z in range(4)] for y in range(4)]
XC_GROUPS = [[x * 8 + zl * 2 + c for x in range(4) for c in range(2)] for zl in range(4)]
ZL_GROUPS = [[x * 8 + zl * 2 + c for zl in range(4)] for x in range(4) for c in range(2)]

NN = (((1,), (0,)), ((), ()))
NT = (((1,), (1,)), ((), ()))
TN = (((0,), (0,)), ((), ()))


def mm(a, b, dims=NN):
    return lax.dot_general(a, b, dims, preferred_element_type=F32)


def whole(n):
    return [pl.BlockSpec(memory_space=pltpu.VMEM)] * n


def params():
    return pltpu.CompilerParams(vmem_limit_bytes=VMEM)


def sds(shape, dtype):
    return jax.ShapeDtypeStruct(shape, dtype)


def low_half(shape):
    return lax.broadcasted_iota(jnp.int32, shape, 1) < FEAT // 2


def of_head(array, head):
    keep = low_half(array.shape)
    zero = jnp.zeros_like(array)
    return jnp.where(keep, array, zero) if head == 0 else jnp.where(keep, zero, array)


def pack_kernel(q_ref, k_ref, v_ref, ids_ref, out_ref):
    ids = jnp.broadcast_to(ids_ref[...].astype(F32), (16, TOK)).astype(BF)
    for d in range(NS):
        cols = slice(d * FEAT, (d + 1) * FEAT)
        out_ref[d, 0:TOK, :] = q_ref[0, :, cols]
        out_ref[d, TOK:2 * TOK, :] = k_ref[0, :, cols]
        out_ref[d, 2 * TOK:3 * TOK, :] = v_ref[0, :, cols]
        out_ref[d, 3 * TOK:ROWS, :] = ids


def selector(x_ref, block):
    parts = []
    for i in range(BLK // TOK):
        ids = x_ref[block * (BLK // TOK) + i, 3 * TOK:ROWS, :].astype(F32)[0:1, :]
        rows = lax.broadcasted_iota(jnp.int32, (PATCHES, TOK), 0).astype(F32)
        parts.append(jnp.where(rows == ids, 1.0, 0.0).astype(BF))
    return jnp.concatenate(parts, axis=1)


def fwd_kernel(x_ref, p_ref, pp_ref, send_ref, acc_ref):
    block = pl.program_id(0)
    step = BLK // TOK

    @pl.when(block == 0)
    def _():
        acc_ref[...] = jnp.zeros_like(acc_ref)

    keys = x_ref[:, TOK:2 * TOK, :].reshape(LEN, FEAT)
    queries = x_ref[pl.ds(block * step, step), 0:TOK, :].reshape(BLK, FEAT)
    queries = (queries.astype(F32) * 0.125).astype(BF)
    sel = selector(x_ref, block)
    for head in range(2):
        scores = mm(of_head(queries, head), keys, NT)
        highest = jnp.max(scores, axis=1, keepdims=True)
        weights = jnp.exp(scores - highest)
        total = jnp.sum(weights, axis=1, keepdims=True)
        probs = (weights * (1.0 / total)).astype(BF)
        p_ref[head] = probs
        acc_ref[head] += mm(sel, probs)

    @pl.when(block == pl.num_programs(0) - 1)
    def _():
        values = x_ref[:, 2 * TOK:3 * TOK, :].reshape(LEN, FEAT)
        pooled = []
        for head in range(2):
            summed = acc_ref[head].astype(BF)
            pp_ref[head] = summed
            pooled.append(mm(summed, values))
        joined = jnp.where(low_half((PATCHES, FEAT)), pooled[0], pooled[1])
        joined = (joined * (1.0 / GROUP)).astype(BF)
        for d in range(NS):
            y = d // NZ
            send_ref[d] = joined[y * PY:(y + 1) * PY, :]


def proj1_kernel(r_ref, win_ref, wout_ref, teacher_ref, pooled_ref, preact_ref, hidden_ref, send_ref):
    for s in range(NS):
        pooled_ref[:, s * FEAT:(s + 1) * FEAT] = r_ref[s]
    pooled = pooled_ref[...]
    partial = None
    for y in range(NY):
        cols = slice(y * FEAT, (y + 1) * FEAT)
        preact = mm(pooled, win_ref[y])
        hidden = (preact * jax.nn.sigmoid(preact)).astype(BF)
        preact_ref[:, cols] = preact
        hidden_ref[:, cols] = hidden
        term = mm(hidden, wout_ref[y])
        partial = term if partial is None else partial + term
    send_ref[0:PY, :] = partial.astype(BF)
    own = teacher_ref[0]
    send_ref[PY:PY + 16, :] = jnp.concatenate([own, own], axis=0)


def proj2_kernel(r_ref, preact_ref, hidden_ref, pooled_ref, win_ref, wout_ref, back_ref, side_ref):
    proj = r_ref[0, 0:PY, :].astype(F32)
    for z in range(1, NZ):
        proj = proj + r_ref[z, 0:PY, :].astype(F32)
    target = jnp.concatenate(
        [r_ref[z, PY:PY + 16, :].astype(F32)[0:8, :] for z in range(NZ)], axis=0
    )
    scale = 1.0 / TEACH
    cross = jnp.sum(proj * target, axis=1, keepdims=True) * scale
    proj_power = jnp.sum(proj * proj, axis=1, keepdims=True) * scale + EPSILON
    teach_power = jnp.sum(target * target, axis=1, keepdims=True) * scale + EPSILON
    grad = (-(target - cross / proj_power * proj) / jnp.sqrt(proj_power * teach_power)).astype(BF)
    pooled = pooled_ref[...]
    terms = None
    for y in range(NY):
        cols = slice(y * FEAT, (y + 1) * FEAT)
        grad_hidden = mm(grad, wout_ref[y], NT)
        preact = preact_ref[:, cols]
        sigma = jax.nn.sigmoid(preact)
        grad_pre = (grad_hidden * sigma * (1.0 + preact * (1.0 - sigma))).astype(BF)
        term = mm(grad_pre, win_ref[y], NT)
        terms = term if terms is None else terms + term
        side_ref[y, :, 0:WIDTH] = pooled
        side_ref[y, :, WIDTH:WIDTH + TEACH] = grad
        side_ref[y, :, WIDTH + TEACH:WIDTH + TEACH + FEAT] = hidden_ref[:, cols]
        side_ref[y, :, WIDTH + TEACH + FEAT:WIDTH + TEACH + 2 * FEAT] = grad_pre
    terms = terms.astype(BF)
    for d in range(NS):
        back_ref[d] = terms[:, d * FEAT:(d + 1) * FEAT]


def bwd_kernel(r_ref, x_ref, pp_ref, p_ref, out_ref, g_ref):
    block = pl.program_id(0)
    step = BLK // TOK

    @pl.when(block == 0)
    def _():
        for y in range(NY):
            summed = r_ref[y * NZ].astype(F32)
            for z in range(1, NZ):
                summed = summed + r_ref[y * NZ + z].astype(F32)
            rounded = summed.astype(BF).astype(F32) * (1.0 / GROUP)
            g_ref[y * PY:(y + 1) * PY, :] = rounded.astype(BF)
        grad = g_ref[...]
        parts = [mm(pp_ref[head], grad, TN) for head in range(2)]
        values_grad = jnp.where(low_half((LEN, FEAT)), parts[0], parts[1]).astype(BF)
        out_ref[:, TOK:2 * TOK, :] = values_grad.reshape(NS, TOK, FEAT)

    keys = x_ref[:, TOK:2 * TOK, :].reshape(LEN, FEAT)
    values = x_ref[:, 2 * TOK:3 * TOK, :].reshape(LEN, FEAT)
    sel = selector(x_ref, block)
    upstream = (mm(sel, g_ref[...], TN) * 0.125).astype(BF)
    parts = []
    for head in range(2):
        dprob = mm(of_head(upstream, head), values, NT)
        probs = p_ref[head].astype(F32)
        delta = jnp.sum(probs * dprob, axis=1, keepdims=True)
        dscore = (probs * (dprob - delta)).astype(BF)
        parts.append(mm(dscore, keys))
    rows = jnp.where(low_half((BLK, FEAT)), parts[0], parts[1]).astype(BF)
    out_ref[pl.ds(block * step, step), 0:TOK, :] = rows.reshape(step, TOK, FEAT)


def weights_kernel(r_ref, out_ref):
    full = [r_ref[y] for y in range(NY)]
    joined = jnp.concatenate(full, axis=0)
    hidden = joined[:, WIDTH + TEACH:WIDTH + TEACH + FEAT]
    grad_pre = joined[:, WIDTH + TEACH + FEAT:WIDTH + TEACH + 2 * FEAT]
    out_ref[0:WIDTH, :] = mm(joined[:, 0:WIDTH], grad_pre, TN).astype(BF)
    grad_out = mm(hidden, joined[:, WIDTH:WIDTH + TEACH], TN).astype(BF)
    for c in range(TEACH // FEAT):
        out_ref[WIDTH + c * FEAT:WIDTH + (c + 1) * FEAT, :] = grad_out[:, c * FEAT:(c + 1) * FEAT]


def unpack_kernel(r_ref, dq_ref, dv_ref):
    for s in range(NS):
        cols = slice(s * FEAT, (s + 1) * FEAT)
        dq_ref[0, :, cols] = r_ref[s, 0:TOK, :]
        dv_ref[0, :, cols] = r_ref[s, TOK:2 * TOK, :]


def exchange(array, axis, groups=None):
    return lax.all_to_all(array, axis, 0, 0, axis_index_groups=groups, tiled=True)


def gather(array, axis, groups=None):
    return lax.all_gather(array, axis, axis=0, axis_index_groups=groups, tiled=False)


def per_device(query, key, value, patch_map, teacher, proj_in, proj_out):
    win = gather(proj_in, "seq", Y_GROUPS)
    wout = gather(proj_out, "seq", Y_GROUPS)

    packed = pl.pallas_call(
        pack_kernel,
        out_shape=sds((NS, ROWS, FEAT), BF),
        in_specs=whole(4),
        out_specs=whole(1)[0],
        compiler_params=params(),
    )(query, key, value, patch_map)
    x = exchange(packed, "seq")

    steps = LEN // BLK
    probs, pooled_probs, pooled_out = pl.pallas_call(
        fwd_kernel,
        grid=(steps,),
        out_shape=(
            sds((2, LEN, LEN), BF),
            sds((2, PATCHES, LEN), BF),
            sds((NS, PY, FEAT), BF),
        ),
        in_specs=[pl.BlockSpec((NS, ROWS, FEAT), lambda i: (0, 0, 0))],
        out_specs=(
            pl.BlockSpec((2, BLK, LEN), lambda i: (0, i, 0)),
            pl.BlockSpec((2, PATCHES, LEN), lambda i: (0, 0, 0)),
            pl.BlockSpec((NS, PY, FEAT), lambda i: (0, 0, 0)),
        ),
        scratch_shapes=[pltpu.VMEM((2, PATCHES, LEN), F32)],
        compiler_params=params(),
    )(x)
    pooled_in = exchange(pooled_out, "seq")

    pooled, preact, hidden, partial = pl.pallas_call(
        proj1_kernel,
        out_shape=(
            sds((PY, WIDTH), BF),
            sds((PY, NY * FEAT), F32),
            sds((PY, NY * FEAT), BF),
            sds((PY + 16, TEACH), BF),
        ),
        in_specs=whole(4),
        out_specs=tuple(whole(4)),
        compiler_params=params(),
    )(pooled_in, win, wout, teacher)
    partials = gather(partial, "seq", Z_GROUPS)

    back, side = pl.pallas_call(
        proj2_kernel,
        out_shape=(
            sds((NS, PY, FEAT), BF),
            sds((NY, PY, WIDTH + TEACH + 2 * FEAT), BF),
        ),
        in_specs=whole(6),
        out_specs=tuple(whole(2)),
        compiler_params=params(),
    )(partials, preact, hidden, pooled, win, wout)
    back_in = exchange(back, "seq")
    side_in = exchange(side, "seq", Y_GROUPS)

    grads = pl.pallas_call(
        bwd_kernel,
        grid=(steps,),
        out_shape=sds((NS, 2 * TOK, FEAT), BF),
        in_specs=[
            pl.BlockSpec((NS, PY, FEAT), lambda i: (0, 0, 0)),
            pl.BlockSpec((NS, ROWS, FEAT), lambda i: (0, 0, 0)),
            pl.BlockSpec((2, PATCHES, LEN), lambda i: (0, 0, 0)),
            pl.BlockSpec((2, BLK, LEN), lambda i: (0, i, 0)),
        ],
        out_specs=pl.BlockSpec((NS, 2 * TOK, FEAT), lambda i: (0, 0, 0)),
        scratch_shapes=[pltpu.VMEM((PATCHES, FEAT), BF)],
        compiler_params=params(),
    )(back_in, x, pooled_probs, probs)
    grads_in = exchange(grads, "seq")

    terms = pl.pallas_call(
        weights_kernel,
        out_shape=sds((WIDTH + TEACH, FEAT), BF),
        in_specs=whole(1),
        out_specs=whole(1)[0],
        compiler_params=params(),
    )(side_in)
    rows = WIDTH + TEACH
    part = exchange(terms.reshape(8, rows // 8, FEAT), "dp", XC_GROUPS)
    part = jnp.sum(part.astype(F32), axis=0).astype(BF)
    part = exchange(part.reshape(4, rows // 32, FEAT), "dp", ZL_GROUPS)
    part = jnp.sum(part.astype(F32), axis=0).astype(BF)
    part = gather(part, "dp", ZL_GROUPS).reshape(rows // 8, FEAT)
    total = gather(part, "dp", XC_GROUPS).reshape(rows, FEAT).astype(F32)
    grad_in = total[:WIDTH]
    grad_out = total[WIDTH:].reshape(TEACH // FEAT, FEAT, FEAT).transpose(1, 0, 2).reshape(FEAT, TEACH)

    grad_query, grad_value = pl.pallas_call(
        unpack_kernel,
        out_shape=(sds((1, TOK, WIDTH), BF), sds((1, TOK, WIDTH), BF)),
        in_specs=whole(1),
        out_specs=tuple(whole(2)),
        compiler_params=params(),
    )(grads_in)
    return (grad_query, grad_value, grad_in, grad_out)


def solution(mesh):
    placed = (
        P("dp", "seq", None),
        P("dp", "seq", None),
        P("dp", "seq", None),
        P("dp", "seq"),
        P("dp", "seq", None),
        P(None, "seq"),
        P("seq", None),
    )
    return jax.shard_map(
        per_device,
        mesh=mesh,
        in_specs=placed,
        out_specs=(P("dp", "seq", None), P("dp", "seq", None), P(None, "seq"), P("seq", None)),
        check_vma=False,
    )
```

```python
import functools

import jax
import jax.numpy as jnp
from jax import lax
from jax.experimental import pallas as pl
from jax.experimental.pallas import tpu as pltpu
from jax.sharding import PartitionSpec as P

BF = jnp.bfloat16
F32 = jnp.float32
NS = 16
NY = 4
NZ = 4
TOK = 128
LEN = 2048
FEAT = 128
PATCHES = 128
PY = 32
TEACH = 1408
WIDTH = 2048
GROUP = 16
EPSILON = 1e-06
ROWS = 2 * TOK + 16
TROWS = 96
EARLY = 4224
LATE = 1408 + 512
ROWS_DP = (2048 + 1408) // 8
FBLK = 512
BBLK = 256
CHUNK = 16
PARTS = 4
MIB = 1024 * 1024

Y_GROUPS = [[y * 4 + z for y in range(4)] for z in range(4)]
Z_GROUPS = [[y * 4 + z for z in range(4)] for y in range(4)]
Y_SHIFT = [[(y * 4 + z, (y + k) % 4 * 4 + z) for y in range(4) for z in range(4)] for k in range(4)]
Z_SHIFT = [[(y * 4 + z, y * 4 + (z + k) % 4) for y in range(4) for z in range(4)] for k in range(4)]
XC_GROUPS = [[x * 8 + zl * 2 + c for x in range(4) for c in range(2)] for zl in range(4)]
ZL_GROUPS = [[x * 8 + zl * 2 + c for zl in range(4)] for x in range(4) for c in range(2)]

NN = (((1,), (0,)), ((), ()))
NT = (((1,), (1,)), ((), ()))
TN = (((0,), (0,)), ((), ()))


def mm(a, b, dims=NN):
    return lax.dot_general(a, b, dims, preferred_element_type=F32)


def whole(n):
    return [pl.BlockSpec(memory_space=pltpu.VMEM)] * n


def params(mib=12):
    return pltpu.CompilerParams(vmem_limit_bytes=mib * MIB)


def sds(shape, dtype):
    return jax.ShapeDtypeStruct(shape, dtype)


def low_half(shape):
    return lax.broadcasted_iota(jnp.int32, shape, 1) < FEAT // 2


def of_head(array, head):
    keep = low_half(array.shape)
    zero = jnp.zeros_like(array)
    return jnp.where(keep, array, zero) if head == 0 else jnp.where(keep, zero, array)


def pack_kernel(q_ref, k_ref, ids_ref, out_ref):
    ids = jnp.broadcast_to(ids_ref[...].astype(F32), (16, TOK)).astype(BF)
    for i in range(NS // PARTS):
        cols = slice(i * FEAT, (i + 1) * FEAT)
        out_ref[i, 0:TOK, :] = q_ref[0, :, cols]
        out_ref[i, TOK:2 * TOK, :] = k_ref[0, :, cols]
        out_ref[i, 2 * TOK:ROWS, :] = ids


def split_value_kernel(v_ref, *out_refs):
    y = lax.axis_index("seq") // NZ
    for k in range(NY):
        for z in range(NZ):
            at = pl.multiple_of((y + k) % NY * (NZ * FEAT) + z * FEAT, FEAT)
            out_refs[k][z] = v_ref[0, :, pl.ds(at, FEAT)]


def turn_value_kernel(a_ref, b_ref, c_ref, d_ref, teacher_ref, *out_refs):
    z = lax.axis_index("seq") % NZ
    own = teacher_ref[0].astype(F32)
    for k in range(NZ):
        for c in range(0, TROWS // 8, 2):
            first = own[:, c * FEAT:(c + 1) * FEAT]
            second = own[:, (c + 1) * FEAT:(c + 2) * FEAT] if (c + 1) * FEAT < TEACH else first
            out_refs[k][c * 8:c * 8 + 16, :] = jnp.concatenate([first, second], axis=0).astype(BF)
        for i, ref in enumerate((a_ref, b_ref, c_ref, d_ref)):
            rows = slice(TROWS + i * TOK, TROWS + (i + 1) * TOK)
            out_refs[k][rows, :] = ref[(z + k) % NZ]


def selector(x_ref, first, count):
    parts = []
    for i in range(count):
        ids = x_ref[first + i, 2 * TOK:ROWS, :].astype(F32)[0:1, :]
        rows = lax.broadcasted_iota(jnp.int32, (PATCHES, TOK), 0).astype(F32)
        parts.append(jnp.where(rows == ids, 1.0, 0.0).astype(BF))
    return jnp.concatenate(parts, axis=1)


def fwd_kernel(x_ref, p_ref, pp_ref, acc_ref, s0_ref, s1_ref):
    block = pl.program_id(0)
    step = FBLK // TOK

    @pl.when(block == 0)
    def _():
        acc_ref[...] = jnp.zeros_like(acc_ref)

    keys = x_ref[:, TOK:2 * TOK, :].reshape(LEN, FEAT)
    queries = x_ref[pl.ds(block * step, step), 0:TOK, :].reshape(FBLK, FEAT)
    queries = (queries.astype(F32) * 0.125).astype(BF)
    sel = selector(x_ref, block * step, step)
    score_refs = (s0_ref, s1_ref)
    for head in range(2):
        score_refs[head][...] = mm(of_head(queries, head), keys, NT)
    for head in range(2):
        for c in range(0, FBLK, CHUNK):
            scores = score_refs[head][c:c + CHUNK, :]
            weights = jnp.exp(scores - jnp.max(scores, axis=1, keepdims=True))
            total = jnp.sum(weights, axis=1, keepdims=True)
            p_ref[head, c:c + CHUNK, :] = (weights * (1.0 / total)).astype(BF)
        acc_ref[head] += mm(sel, p_ref[head])

    @pl.when(block == pl.num_programs(0) - 1)
    def _():
        for head in range(2):
            pp_ref[head] = acc_ref[head].astype(BF)


def pool_kernel(pp_ref, a_ref, b_ref, c_ref, d_ref, send_ref, v_ref, target_ref):
    y = lax.axis_index("seq") // NZ
    z = lax.axis_index("seq") % NZ
    for k, ref in enumerate((a_ref, b_ref, c_ref, d_ref)):
        source = (z + NZ - k) % NZ
        for i in range(NY):
            v_ref[(y + NY - i) % NY * NZ + source] = ref[TROWS + i * TOK:TROWS + (i + 1) * TOK, :]
        at = pl.ds(pl.multiple_of(source * 8, 8), 8)
        for c in range(0, TROWS // 8, 2):
            pair = ref[c * 8:c * 8 + 16, :].astype(F32)
            target_ref[at, c * FEAT:(c + 1) * FEAT] = pair[0:8, :]
            if (c + 1) * FEAT < TEACH:
                target_ref[at, (c + 1) * FEAT:(c + 2) * FEAT] = pair[8:16, :]
    values = v_ref[...].reshape(LEN, FEAT)
    pooled = [mm(pp_ref[head], values) for head in range(2)]
    joined = jnp.where(low_half((PATCHES, FEAT)), pooled[0], pooled[1])
    joined = (joined * (1.0 / GROUP)).astype(BF)
    for d in range(NS):
        send_ref[d] = joined[d // NZ * PY:(d // NZ + 1) * PY, :]


def proj1_kernel(r_ref, win_ref, wout_ref, early_ref, preact_ref, send_ref, acc_ref):
    y = pl.program_id(0)

    @pl.when(y == 0)
    def _():
        for s in range(NS):
            early_ref[:, s * FEAT:(s + 1) * FEAT] = r_ref[s]
        early_ref[:, WIDTH + NY * FEAT:EARLY] = jnp.zeros((PY, EARLY - WIDTH - NY * FEAT), BF)
        acc_ref[...] = jnp.zeros_like(acc_ref)

    preact = mm(early_ref[:, 0:WIDTH], win_ref[0])
    hidden = (preact * jax.nn.sigmoid(preact)).astype(BF)
    preact_ref[...] = preact
    early_ref[:, pl.ds(pl.multiple_of(WIDTH + y * FEAT, FEAT), FEAT)] = hidden
    acc_ref[...] += mm(hidden, wout_ref[0])

    @pl.when(y == NY - 1)
    def _():
        send_ref[...] = acc_ref[...].astype(BF)


def proj2_kernel(
    r_ref, target_ref, preact_ref, win_ref, wout_ref, back_ref, late_ref, terms_ref
):
    y = pl.program_id(0)

    @pl.when(y == 0)
    def _():
        proj = r_ref[0].astype(F32)
        for z in range(1, NZ):
            proj = proj + r_ref[z].astype(F32)
        target = target_ref[...]
        scale = 1.0 / TEACH
        cross = jnp.sum(proj * target, axis=1, keepdims=True) * scale
        proj_power = jnp.sum(proj * proj, axis=1, keepdims=True) * scale + EPSILON
        teach_power = jnp.sum(target * target, axis=1, keepdims=True) * scale + EPSILON
        grad = -(target - cross / proj_power * proj) / jnp.sqrt(proj_power * teach_power)
        late_ref[:, 0:TEACH] = grad.astype(BF)
        terms_ref[...] = jnp.zeros_like(terms_ref)

    grad_hidden = mm(late_ref[:, 0:TEACH], wout_ref[0], NT)
    preact = preact_ref[...]
    sigma = jax.nn.sigmoid(preact)
    grad_pre = (grad_hidden * sigma * (1.0 + preact * (1.0 - sigma))).astype(BF)
    terms_ref[...] += mm(grad_pre, win_ref[0], NT)
    late_ref[:, pl.ds(pl.multiple_of(TEACH + y * FEAT, FEAT), FEAT)] = grad_pre

    @pl.when(y == NY - 1)
    def _():
        terms = terms_ref[...].astype(BF)
        for d in range(NS):
            back_ref[d] = terms[:, d * FEAT:(d + 1) * FEAT]


def value_grad_kernel(r_ref, pp_ref, g_ref, *out_refs):
    z = lax.axis_index("seq") % NZ
    for y in range(NY):
        summed = r_ref[y * NZ].astype(F32)
        for k in range(1, NZ):
            summed = summed + r_ref[y * NZ + k].astype(F32)
        rounded = summed.astype(BF).astype(F32) * (1.0 / GROUP)
        g_ref[y * PY:(y + 1) * PY, :] = rounded.astype(BF)
    grad = g_ref[...]
    for k in range(NZ):
        for y in range(NY):
            at = pl.multiple_of((y * NZ + (z + k) % NZ) * TOK, TOK)
            parts = [mm(pp_ref[head, :, pl.ds(at, TOK)], grad, TN) for head in range(2)]
            out_refs[k][y] = jnp.where(low_half((TOK, FEAT)), parts[0], parts[1]).astype(BF)


def turn_grad_kernel(a_ref, b_ref, c_ref, d_ref, *out_refs):
    y = lax.axis_index("seq") // NZ
    for j in range(NY):
        for k, ref in enumerate((a_ref, b_ref, c_ref, d_ref)):
            out_refs[j][k] = ref[(y + j) % NY]


def join_grad_kernel(a_ref, b_ref, c_ref, d_ref, out_ref):
    y = lax.axis_index("seq") // NZ
    z = lax.axis_index("seq") % NZ
    for j, ref in enumerate((a_ref, b_ref, c_ref, d_ref)):
        for k in range(NZ):
            source = (y + NY - j) % NY * NZ + (z + NZ - k) % NZ
            out_ref[0, :, pl.ds(pl.multiple_of(source * FEAT, FEAT), FEAT)] = ref[k]


def bwd_kernel(g_ref, x_ref, v_ref, p_ref, out_ref, d0_ref, d1_ref, w0_ref, w1_ref):
    block = pl.program_id(0)
    step = BBLK // TOK
    keys = x_ref[:, TOK:2 * TOK, :].reshape(LEN, FEAT)
    values = v_ref[...].reshape(LEN, FEAT)
    sel = selector(x_ref, block * step, step)
    upstream = (mm(sel, g_ref[...], TN) * 0.125).astype(BF)
    dprob_refs, work_refs = (d0_ref, d1_ref), (w0_ref, w1_ref)
    for head in range(2):
        dprob_refs[head][...] = mm(of_head(upstream, head), values, NT)
    parts = []
    for head in range(2):
        for c in range(0, BBLK, CHUNK):
            probs = p_ref[head, c:c + CHUNK, :].astype(F32)
            dprob = dprob_refs[head][c:c + CHUNK, :]
            delta = jnp.sum(probs * dprob, axis=1, keepdims=True)
            work_refs[head][c:c + CHUNK, :] = (probs * (dprob - delta)).astype(BF)
        parts.append(mm(work_refs[head][...], keys))
    rows = jnp.where(low_half((BBLK, FEAT)), parts[0], parts[1]).astype(BF)
    out_ref[...] = rows.reshape(step, TOK, FEAT)


def weights_kernel(early_ref, late_ref, out_ref):
    y = lax.axis_index("seq") // NZ
    at = pl.multiple_of(WIDTH + y * FEAT, FEAT)
    hidden = early_ref[:, :, pl.ds(at, FEAT)].reshape(PATCHES, FEAT)
    at = pl.multiple_of(TEACH + y * FEAT, FEAT)
    grad_pre = late_ref[:, :, pl.ds(at, FEAT)].reshape(PATCHES, FEAT)
    pooled = early_ref[:, :, 0:WIDTH].reshape(PATCHES, WIDTH)
    grad = late_ref[:, :, 0:TEACH].reshape(PATCHES, TEACH)
    out_ref[0:WIDTH, :] = mm(pooled, grad_pre, TN).astype(BF)
    grad_out = mm(hidden, grad, TN).astype(BF)
    for c in range(TEACH // FEAT):
        out_ref[WIDTH + c * FEAT:WIDTH + (c + 1) * FEAT, :] = grad_out[:, c * FEAT:(c + 1) * FEAT]


def sum_kernel(r_ref, out_ref):
    total = r_ref[0].astype(F32)
    for k in range(1, r_ref.shape[0]):
        total = total + r_ref[k].astype(F32)
    out_ref[...] = total.astype(BF)


def finish_kernel(r_ref, in_ref, out_ref):
    in_ref[...] = r_ref[0:WIDTH, :].astype(F32)
    for c in range(TEACH // FEAT):
        block = r_ref[WIDTH + c * FEAT:WIDTH + (c + 1) * FEAT, :]
        out_ref[:, c * FEAT:(c + 1) * FEAT] = block.astype(F32)


def unpack_kernel(r_ref, dq_ref):
    for i in range(NS // PARTS):
        dq_ref[0, :, i * FEAT:(i + 1) * FEAT] = r_ref[i]


def exchange(array, axis, groups=None):
    return lax.all_to_all(array, axis, 0, 0, axis_index_groups=groups, tiled=True)


def gather(array, axis, groups=None):
    return lax.all_gather(array, axis, axis=0, axis_index_groups=groups, tiled=False)


def fixed(shape):
    return pl.BlockSpec(shape, lambda i: (0,) * len(shape))


def per_device(query, key, value, patch_map, teacher, proj_in, proj_out):
    win = gather(proj_in, "seq", Y_GROUPS)
    wout = gather(proj_out, "seq", Y_GROUPS)
    columns = pl.BlockSpec((1, TOK, WIDTH // PARTS), lambda i: (0, 0, i))
    chunk = lambda rows: pl.BlockSpec((NS // PARTS, rows, FEAT), lambda i: (i, 0, 0))

    packed = pl.pallas_call(
        pack_kernel,
        grid=(PARTS,),
        out_shape=sds((NS, ROWS, FEAT), BF),
        in_specs=[columns, columns, fixed((1, TOK))],
        out_specs=chunk(ROWS),
        compiler_params=params(59),
    )(query, key, patch_map)
    packed, value, teacher = lax.optimization_barrier((packed, value, teacher))
    x = exchange(packed, "seq")
    pieces = pl.pallas_call(
        split_value_kernel,
        out_shape=(sds((NZ, TOK, FEAT), BF),) * NY,
        in_specs=whole(1),
        out_specs=tuple(whole(NY)),
        compiler_params=params(),
    )(value)
    pieces = [pieces[0]] + [lax.ppermute(pieces[k], "seq", Y_SHIFT[k]) for k in range(1, NY)]
    turned = pl.pallas_call(
        turn_value_kernel,
        out_shape=(sds((TROWS + NY * TOK, FEAT), BF),) * NZ,
        in_specs=whole(5),
        out_specs=tuple(whole(NZ)),
        compiler_params=params(),
    )(*pieces, teacher)
    turned = [turned[0]] + [lax.ppermute(turned[k], "seq", Z_SHIFT[k]) for k in range(1, NZ)]

    probs, pooled_probs = pl.pallas_call(
        fwd_kernel,
        grid=(LEN // FBLK,),
        out_shape=(sds((2, LEN, LEN), BF), sds((2, PATCHES, LEN), BF)),
        in_specs=[fixed((NS, ROWS, FEAT))],
        out_specs=(
            pl.BlockSpec((2, FBLK, LEN), lambda i: (0, i, 0)),
            fixed((2, PATCHES, LEN)),
        ),
        scratch_shapes=[
            pltpu.VMEM((2, PATCHES, LEN), F32),
            pltpu.VMEM((FBLK, LEN), F32),
            pltpu.VMEM((FBLK, LEN), F32),
        ],
        compiler_params=params(40),
        cost_estimate=pl.CostEstimate(flops=10 ** 6, bytes_accessed=10 ** 6, transcendentals=0),
    )(x)
    pooled_out, values, targets = pl.pallas_call(
        pool_kernel,
        out_shape=(sds((NS, PY, FEAT), BF), sds((NS, TOK, FEAT), BF), sds((PY, TEACH), F32)),
        in_specs=whole(5),
        out_specs=tuple(whole(3)),
        compiler_params=params(),
    )(pooled_probs, *turned)
    pooled_in = exchange(pooled_out, "seq")

    win_spec = pl.BlockSpec((1, WIDTH, FEAT), lambda i: (i, 0, 0))
    wout_spec = pl.BlockSpec((1, FEAT, TEACH), lambda i: (i, 0, 0))
    slab = pl.BlockSpec((PY, FEAT), lambda i: (0, i))
    early, preact, partial = pl.pallas_call(
        proj1_kernel,
        grid=(NY,),
        out_shape=(sds((PY, EARLY), BF), sds((PY, NY * FEAT), F32), sds((PY, TEACH), BF)),
        in_specs=[fixed((NS, PY, FEAT)), win_spec, wout_spec],
        out_specs=(fixed((PY, EARLY)), slab, fixed((PY, TEACH))),
        scratch_shapes=[pltpu.VMEM((PY, TEACH), F32)],
        compiler_params=params(59),
    )(pooled_in, win, wout)
    early_in = gather(early, "seq", Y_GROUPS)
    partials = gather(partial, "seq", Z_GROUPS)

    back, late = pl.pallas_call(
        proj2_kernel,
        grid=(NY,),
        out_shape=(sds((NS, PY, FEAT), BF), sds((PY, LATE), BF)),
        in_specs=[fixed((NZ, PY, TEACH)), fixed((PY, TEACH)), slab, win_spec, wout_spec],
        out_specs=(fixed((NS, PY, FEAT)), fixed((PY, LATE))),
        scratch_shapes=[pltpu.VMEM((PY, WIDTH), F32)],
        compiler_params=params(),
    )(partials, targets, preact, win, wout)
    back_in = exchange(back, "seq")
    late_in = gather(late, "seq", Y_GROUPS)

    terms = pl.pallas_call(
        weights_kernel,
        out_shape=sds((WIDTH + TEACH, FEAT), BF),
        in_specs=whole(2),
        out_specs=whole(1)[0],
        compiler_params=params(),
    )(early_in, late_in)
    terms, back_in = lax.optimization_barrier((terms, back_in))
    part = exchange(terms.reshape(8, ROWS_DP, FEAT), "dp", XC_GROUPS)

    grad_rows, *moved = pl.pallas_call(
        value_grad_kernel,
        out_shape=(sds((PATCHES, FEAT), BF),) + (sds((NY, TOK, FEAT), BF),) * NZ,
        in_specs=whole(2),
        out_specs=tuple(whole(1 + NZ)),
        compiler_params=params(),
    )(back_in, pooled_probs)
    moved = [moved[0]] + [lax.ppermute(moved[k], "seq", Z_SHIFT[k]) for k in range(1, NZ)]
    grads = pl.pallas_call(
        bwd_kernel,
        grid=(LEN // BBLK,),
        out_shape=sds((NS, TOK, FEAT), BF),
        in_specs=[
            fixed((PATCHES, FEAT)),
            fixed((NS, ROWS, FEAT)),
            fixed((NS, TOK, FEAT)),
            pl.BlockSpec((2, BBLK, LEN), lambda i: (0, i, 0)),
        ],
        out_specs=pl.BlockSpec((BBLK // TOK, TOK, FEAT), lambda i: (i, 0, 0)),
        scratch_shapes=[
            pltpu.VMEM((BBLK, LEN), F32),
            pltpu.VMEM((BBLK, LEN), F32),
            pltpu.VMEM((BBLK, LEN), BF),
            pltpu.VMEM((BBLK, LEN), BF),
        ],
        compiler_params=params(50),
        cost_estimate=pl.CostEstimate(flops=10 ** 10, bytes_accessed=2 * 10 ** 7, transcendentals=0),
    )(grad_rows, x, values, probs)
    turned = pl.pallas_call(
        turn_grad_kernel,
        out_shape=(sds((NZ, TOK, FEAT), BF),) * NY,
        in_specs=whole(NZ),
        out_specs=tuple(whole(NY)),
        compiler_params=params(),
    )(*moved)
    turned, grads = lax.optimization_barrier((turned, grads))
    turned = [turned[0]] + [lax.ppermute(turned[k], "seq", Y_SHIFT[k]) for k in range(1, NY)]
    grad_value = pl.pallas_call(
        join_grad_kernel,
        out_shape=sds((1, TOK, WIDTH), BF),
        in_specs=whole(NY),
        out_specs=whole(1)[0],
        compiler_params=params(),
    )(*turned)
    part, grads = lax.optimization_barrier((part, grads))
    part = pl.pallas_call(
        sum_kernel,
        out_shape=sds((ROWS_DP, FEAT), BF),
        in_specs=whole(1),
        out_specs=whole(1)[0],
        compiler_params=params(),
    )(part)
    part = gather(part, "dp", ZL_GROUPS)
    part, grads = lax.optimization_barrier((part, grads))
    grads_in = exchange(grads, "seq")
    part = pl.pallas_call(
        sum_kernel,
        out_shape=sds((ROWS_DP, FEAT), BF),
        in_specs=whole(1),
        out_specs=whole(1)[0],
        compiler_params=params(),
    )(part)
    total = gather(part, "dp", XC_GROUPS).reshape(WIDTH + TEACH, FEAT)
    grad_in, grad_out = pl.pallas_call(
        finish_kernel,
        out_shape=(sds((WIDTH, FEAT), F32), sds((FEAT, TEACH), F32)),
        in_specs=whole(1),
        out_specs=tuple(whole(2)),
        compiler_params=params(),
    )(total)

    grad_query = pl.pallas_call(
        unpack_kernel,
        grid=(PARTS,),
        out_shape=sds((1, TOK, WIDTH), BF),
        in_specs=[chunk(TOK)],
        out_specs=columns,
        compiler_params=params(),
    )(grads_in)
    return (grad_query, grad_value, grad_in, grad_out)


def solution(mesh):
    placed = (
        P("dp", "seq", None),
        P("dp", "seq", None),
        P("dp", "seq", None),
        P("dp", "seq"),
        P("dp", "seq", None),
        P(None, "seq"),
        P("seq", None),
    )
    return jax.shard_map(
        per_device,
        mesh=mesh,
        in_specs=placed,
        out_specs=(P("dp", "seq", None), P("dp", "seq", None), P(None, "seq"), P("seq", None)),
        check_vma=False,
    )
```

```python
import functools

import jax
import jax.numpy as jnp
from jax import lax
from jax.experimental import pallas as pl
from jax.experimental.pallas import tpu as pltpu
from jax.sharding import PartitionSpec as P

BF = jnp.bfloat16
F32 = jnp.float32
NS = 16
NY = 4
NZ = 4
TOK = 128
LEN = 2048
FEAT = 128
PATCHES = 128
PY = 32
TEACH = 1408
WIDTH = 2048
GROUP = 16
EPSILON = 1e-06
ROWS = 2 * TOK + 16
TROWS = 96
EARLY = 4224
LATE = 1408 + 512
ROWS_DP = (2048 + 1408) // 8
FBLK = 512
BBLK = 256
CHUNK = 16
PARTS = 4
MIB = 1024 * 1024

Y_GROUPS = [[y * 4 + z for y in range(4)] for z in range(4)]
Z_GROUPS = [[y * 4 + z for z in range(4)] for y in range(4)]
Y_SHIFT = [[(y * 4 + z, (y + k) % 4 * 4 + z) for y in range(4) for z in range(4)] for k in range(4)]
Z_SHIFT = [[(y * 4 + z, y * 4 + (z + k) % 4) for y in range(4) for z in range(4)] for k in range(4)]
XC_GROUPS = [[x * 8 + zl * 2 + c for x in range(4) for c in range(2)] for zl in range(4)]
ZL_GROUPS = [[x * 8 + zl * 2 + c for zl in range(4)] for x in range(4) for c in range(2)]

NN = (((1,), (0,)), ((), ()))
NT = (((1,), (1,)), ((), ()))
TN = (((0,), (0,)), ((), ()))


def mm(a, b, dims=NN):
    return lax.dot_general(a, b, dims, preferred_element_type=F32)


def whole(n):
    return [pl.BlockSpec(memory_space=pltpu.VMEM)] * n


def params(mib=12):
    return pltpu.CompilerParams(vmem_limit_bytes=mib * MIB)


def sds(shape, dtype):
    return jax.ShapeDtypeStruct(shape, dtype)


def low_half(shape):
    return lax.broadcasted_iota(jnp.int32, shape, 1) < FEAT // 2


def of_head(array, head):
    keep = low_half(array.shape)
    zero = jnp.zeros_like(array)
    return jnp.where(keep, array, zero) if head == 0 else jnp.where(keep, zero, array)


def pack_kernel(q_ref, k_ref, ids_ref, out_ref):
    ids = jnp.broadcast_to(ids_ref[...].astype(F32), (16, TOK)).astype(BF)
    for i in range(NS // PARTS):
        cols = slice(i * FEAT, (i + 1) * FEAT)
        out_ref[i, 0:TOK, :] = q_ref[0, :, cols]
        out_ref[i, TOK:2 * TOK, :] = k_ref[0, :, cols]
        out_ref[i, 2 * TOK:ROWS, :] = ids


def split_value_kernel(v_ref, *out_refs):
    y = lax.axis_index("seq") // NZ
    for k in range(NY):
        for z in range(NZ):
            at = pl.multiple_of((y + k) % NY * (NZ * FEAT) + z * FEAT, FEAT)
            out_refs[k][z] = v_ref[0, :, pl.ds(at, FEAT)]


def turn_value_kernel(a_ref, b_ref, c_ref, d_ref, teacher_ref, *out_refs):
    z = lax.axis_index("seq") % NZ
    own = teacher_ref[0].astype(F32)
    for k in range(NZ):
        for c in range(0, TROWS // 8, 2):
            first = own[:, c * FEAT:(c + 1) * FEAT]
            second = own[:, (c + 1) * FEAT:(c + 2) * FEAT] if (c + 1) * FEAT < TEACH else first
            out_refs[k][c * 8:c * 8 + 16, :] = jnp.concatenate([first, second], axis=0).astype(BF)
        for i, ref in enumerate((a_ref, b_ref, c_ref, d_ref)):
            rows = slice(TROWS + i * TOK, TROWS + (i + 1) * TOK)
            out_refs[k][rows, :] = ref[(z + k) % NZ]


def selector(x_ref, first, count):
    parts = []
    for i in range(count):
        ids = x_ref[first + i, 2 * TOK:ROWS, :].astype(F32)[0:1, :]
        rows = lax.broadcasted_iota(jnp.int32, (PATCHES, TOK), 0).astype(F32)
        parts.append(jnp.where(rows == ids, 1.0, 0.0).astype(BF))
    return jnp.concatenate(parts, axis=1)


def fwd_kernel(x_ref, p_ref, pp_ref, acc_ref, s0_ref, s1_ref):
    block = pl.program_id(0)
    step = FBLK // TOK

    @pl.when(block == 0)
    def _():
        acc_ref[...] = jnp.zeros_like(acc_ref)

    keys = x_ref[:, TOK:2 * TOK, :].reshape(LEN, FEAT)
    queries = x_ref[pl.ds(block * step, step), 0:TOK, :].reshape(FBLK, FEAT)
    queries = (queries.astype(F32) * 0.125).astype(BF)
    sel = selector(x_ref, block * step, step)
    score_refs = (s0_ref, s1_ref)
    for head in range(2):
        score_refs[head][...] = mm(of_head(queries, head), keys, NT)
    for head in range(2):
        for c in range(0, FBLK, CHUNK):
            scores = score_refs[head][c:c + CHUNK, :]
            weights = jnp.exp(scores - jnp.max(scores, axis=1, keepdims=True))
            total = jnp.sum(weights, axis=1, keepdims=True)
            p_ref[head, c:c + CHUNK, :] = (weights * (1.0 / total)).astype(BF)
        acc_ref[head] += mm(sel, p_ref[head])

    @pl.when(block == pl.num_programs(0) - 1)
    def _():
        for head in range(2):
            pp_ref[head] = acc_ref[head].astype(BF)


def pool_kernel(pp_ref, a_ref, b_ref, c_ref, d_ref, send_ref, v_ref, target_ref):
    y = lax.axis_index("seq") // NZ
    z = lax.axis_index("seq") % NZ
    for k, ref in enumerate((a_ref, b_ref, c_ref, d_ref)):
        source = (z + NZ - k) % NZ
        for i in range(NY):
            v_ref[(y + NY - i) % NY * NZ + source] = ref[TROWS + i * TOK:TROWS + (i + 1) * TOK, :]
        at = pl.ds(pl.multiple_of(source * 8, 8), 8)
        for c in range(0, TROWS // 8, 2):
            pair = ref[c * 8:c * 8 + 16, :].astype(F32)
            target_ref[at, c * FEAT:(c + 1) * FEAT] = pair[0:8, :]
            if (c + 1) * FEAT < TEACH:
                target_ref[at, (c + 1) * FEAT:(c + 2) * FEAT] = pair[8:16, :]
    values = v_ref[...].reshape(LEN, FEAT)
    pooled = [mm(pp_ref[head], values) for head in range(2)]
    joined = jnp.where(low_half((PATCHES, FEAT)), pooled[0], pooled[1])
    joined = (joined * (1.0 / GROUP)).astype(BF)
    for d in range(NS):
        send_ref[d] = joined[d // NZ * PY:(d // NZ + 1) * PY, :]


def hold_kernel(a_ref, b_ref, a_out, b_out, sems):
    first = pltpu.make_async_copy(a_ref, a_out, sems.at[0])
    second = pltpu.make_async_copy(b_ref, b_out, sems.at[1])
    first.start()
    second.start()
    first.wait()
    second.wait()


def proj1_kernel(r_ref, win_ref, wout_ref, early_ref, preact_ref, send_ref, acc_ref):
    y = pl.program_id(0)

    @pl.when(y == 0)
    def _():
        for s in range(NS):
            early_ref[:, s * FEAT:(s + 1) * FEAT] = r_ref[s]
        early_ref[:, WIDTH + NY * FEAT:EARLY] = jnp.zeros((PY, EARLY - WIDTH - NY * FEAT), BF)
        acc_ref[...] = jnp.zeros_like(acc_ref)

    preact = mm(early_ref[:, 0:WIDTH], win_ref[0])
    hidden = (preact * jax.nn.sigmoid(preact)).astype(BF)
    preact_ref[...] = preact
    early_ref[:, pl.ds(pl.multiple_of(WIDTH + y * FEAT, FEAT), FEAT)] = hidden
    acc_ref[...] += mm(hidden, wout_ref[0])

    @pl.when(y == NY - 1)
    def _():
        send_ref[...] = acc_ref[...].astype(BF)


def proj2_kernel(
    r_ref, target_ref, preact_ref, win_ref, wout_ref, back_ref, late_ref, terms_ref
):
    y = pl.program_id(0)

    @pl.when(y == 0)
    def _():
        proj = r_ref[0].astype(F32)
        for z in range(1, NZ):
            proj = proj + r_ref[z].astype(F32)
        target = target_ref[...]
        scale = 1.0 / TEACH
        cross = jnp.sum(proj * target, axis=1, keepdims=True) * scale
        proj_power = jnp.sum(proj * proj, axis=1, keepdims=True) * scale + EPSILON
        teach_power = jnp.sum(target * target, axis=1, keepdims=True) * scale + EPSILON
        grad = -(target - cross / proj_power * proj) / jnp.sqrt(proj_power * teach_power)
        late_ref[:, 0:TEACH] = grad.astype(BF)
        terms_ref[...] = jnp.zeros_like(terms_ref)

    grad_hidden = mm(late_ref[:, 0:TEACH], wout_ref[0], NT)
    preact = preact_ref[...]
    sigma = jax.nn.sigmoid(preact)
    grad_pre = (grad_hidden * sigma * (1.0 + preact * (1.0 - sigma))).astype(BF)
    terms_ref[...] += mm(grad_pre, win_ref[0], NT)
    late_ref[:, pl.ds(pl.multiple_of(TEACH + y * FEAT, FEAT), FEAT)] = grad_pre

    @pl.when(y == NY - 1)
    def _():
        terms = terms_ref[...].astype(BF)
        for d in range(NS):
            back_ref[d] = terms[:, d * FEAT:(d + 1) * FEAT]


def value_grad_kernel(r_ref, pp_ref, g_ref, *out_refs):
    z = lax.axis_index("seq") % NZ
    for y in range(NY):
        summed = r_ref[y * NZ].astype(F32)
        for k in range(1, NZ):
            summed = summed + r_ref[y * NZ + k].astype(F32)
        rounded = summed.astype(BF).astype(F32) * (1.0 / GROUP)
        g_ref[y * PY:(y + 1) * PY, :] = rounded.astype(BF)
    grad = g_ref[...]
    for k in range(NZ):
        for y in range(NY):
            at = pl.multiple_of((y * NZ + (z + k) % NZ) * TOK, TOK)
            parts = [mm(pp_ref[head, :, pl.ds(at, TOK)], grad, TN) for head in range(2)]
            out_refs[k][y] = jnp.where(low_half((TOK, FEAT)), parts[0], parts[1]).astype(BF)


def stack_grad_kernel(a_ref, b_ref, c_ref, d_ref, out_ref):
    for k, ref in enumerate((a_ref, b_ref, c_ref, d_ref)):
        out_ref[k] = ref[...]


def join_grad_kernel(r_ref, out_ref, held_ref, sems):
    y = lax.axis_index("seq") // NZ
    z = lax.axis_index("seq") % NZ
    copies = []
    for source in range(NY):
        for k in range(NZ):
            n = source * NZ + k
            copies.append(pltpu.make_async_copy(r_ref.at[source, k, y], held_ref.at[n], sems.at[n]))
            copies[-1].start()
    for copy in copies:
        copy.wait()
    for source in range(NY):
        for k in range(NZ):
            at = pl.multiple_of((source * NZ + (z + NZ - k) % NZ) * FEAT, FEAT)
            out_ref[0, :, pl.ds(at, FEAT)] = held_ref[source * NZ + k]


def bwd_kernel(g_ref, x_ref, v_ref, p_ref, out_ref, d0_ref, d1_ref, w0_ref, w1_ref):
    block = pl.program_id(0)
    step = BBLK // TOK
    keys = x_ref[:, TOK:2 * TOK, :].reshape(LEN, FEAT)
    values = v_ref[...].reshape(LEN, FEAT)
    sel = selector(x_ref, block * step, step)
    upstream = (mm(sel, g_ref[...], TN) * 0.125).astype(BF)
    dprob_refs, work_refs = (d0_ref, d1_ref), (w0_ref, w1_ref)
    for head in range(2):
        dprob_refs[head][...] = mm(of_head(upstream, head), values, NT)
    parts = []
    for head in range(2):
        for c in range(0, BBLK, CHUNK):
            probs = p_ref[head, c:c + CHUNK, :].astype(F32)
            dprob = dprob_refs[head][c:c + CHUNK, :]
            delta = jnp.sum(probs * dprob, axis=1, keepdims=True)
            work_refs[head][c:c + CHUNK, :] = (probs * (dprob - delta)).astype(BF)
        parts.append(mm(work_refs[head][...], keys))
    rows = jnp.where(low_half((BBLK, FEAT)), parts[0], parts[1]).astype(BF)
    out_ref[...] = rows.reshape(step, TOK, FEAT)


def weights_kernel(early_ref, late_ref, out_ref):
    y = lax.axis_index("seq") // NZ
    at = pl.multiple_of(WIDTH + y * FEAT, FEAT)
    hidden = early_ref[:, :, pl.ds(at, FEAT)].reshape(PATCHES, FEAT)
    at = pl.multiple_of(TEACH + y * FEAT, FEAT)
    grad_pre = late_ref[:, :, pl.ds(at, FEAT)].reshape(PATCHES, FEAT)
    pooled = early_ref[:, :, 0:WIDTH].reshape(PATCHES, WIDTH)
    grad = late_ref[:, :, 0:TEACH].reshape(PATCHES, TEACH)
    out_ref[0:WIDTH, :] = mm(pooled, grad_pre, TN).astype(BF)
    grad_out = mm(hidden, grad, TN).astype(BF)
    for c in range(TEACH // FEAT):
        out_ref[WIDTH + c * FEAT:WIDTH + (c + 1) * FEAT, :] = grad_out[:, c * FEAT:(c + 1) * FEAT]


def sum_kernel(r_ref, out_ref):
    total = r_ref[0].astype(F32)
    for k in range(1, r_ref.shape[0]):
        total = total + r_ref[k].astype(F32)
    out_ref[...] = total.astype(BF)


def finish_kernel(r_ref, in_ref, out_ref):
    in_ref[...] = r_ref[0:WIDTH, :].astype(F32)
    for c in range(TEACH // FEAT):
        block = r_ref[WIDTH + c * FEAT:WIDTH + (c + 1) * FEAT, :]
        out_ref[:, c * FEAT:(c + 1) * FEAT] = block.astype(F32)


def unpack_kernel(r_ref, dq_ref):
    for i in range(NS // PARTS):
        dq_ref[0, :, i * FEAT:(i + 1) * FEAT] = r_ref[i]


def exchange(array, axis, groups=None):
    return lax.all_to_all(array, axis, 0, 0, axis_index_groups=groups, tiled=True)


def gather(array, axis, groups=None):
    return lax.all_gather(array, axis, axis=0, axis_index_groups=groups, tiled=False)


def fixed(shape):
    return pl.BlockSpec(shape, lambda i: (0,) * len(shape))


def per_device(query, key, value, patch_map, teacher, proj_in, proj_out):
    win = gather(proj_in, "seq", Y_GROUPS)
    wout = gather(proj_out, "seq", Y_GROUPS)
    columns = pl.BlockSpec((1, TOK, WIDTH // PARTS), lambda i: (0, 0, i))
    chunk = lambda rows: pl.BlockSpec((NS // PARTS, rows, FEAT), lambda i: (i, 0, 0))

    packed = pl.pallas_call(
        pack_kernel,
        grid=(PARTS,),
        out_shape=sds((NS, ROWS, FEAT), BF),
        in_specs=[columns, columns, fixed((1, TOK))],
        out_specs=chunk(ROWS),
        compiler_params=params(59),
    )(query, key, patch_map)
    packed, value, teacher = lax.optimization_barrier((packed, value, teacher))
    x = exchange(packed, "seq")
    pieces = pl.pallas_call(
        split_value_kernel,
        out_shape=(sds((NZ, TOK, FEAT), BF),) * NY,
        in_specs=whole(1),
        out_specs=tuple(whole(NY)),
        compiler_params=params(),
    )(value)
    pieces = [pieces[0]] + [lax.ppermute(pieces[k], "seq", Y_SHIFT[k]) for k in range(1, NY)]
    turned = pl.pallas_call(
        turn_value_kernel,
        out_shape=(sds((TROWS + NY * TOK, FEAT), BF),) * NZ,
        in_specs=whole(5),
        out_specs=tuple(whole(NZ)),
        compiler_params=params(),
    )(*pieces, teacher)
    turned = [turned[0]] + [lax.ppermute(turned[k], "seq", Z_SHIFT[k]) for k in range(1, NZ)]

    probs, pooled_probs = pl.pallas_call(
        fwd_kernel,
        grid=(LEN // FBLK,),
        out_shape=(sds((2, LEN, LEN), BF), sds((2, PATCHES, LEN), BF)),
        in_specs=[fixed((NS, ROWS, FEAT))],
        out_specs=(
            pl.BlockSpec((2, FBLK, LEN), lambda i: (0, i, 0)),
            fixed((2, PATCHES, LEN)),
        ),
        scratch_shapes=[
            pltpu.VMEM((2, PATCHES, LEN), F32),
            pltpu.VMEM((FBLK, LEN), F32),
            pltpu.VMEM((FBLK, LEN), F32),
        ],
        compiler_params=params(40),
        cost_estimate=pl.CostEstimate(flops=10 ** 6, bytes_accessed=10 ** 6, transcendentals=0),
    )(x)
    pooled_out, values, targets = pl.pallas_call(
        pool_kernel,
        out_shape=(sds((NS, PY, FEAT), BF), sds((NS, TOK, FEAT), BF), sds((PY, TEACH), F32)),
        in_specs=whole(5),
        out_specs=tuple(whole(3)),
        compiler_params=params(),
    )(pooled_probs, *turned)
    win, wout, pooled_out = lax.optimization_barrier((win, wout, pooled_out))
    pooled_in = exchange(pooled_out, "seq")
    win, wout = pl.pallas_call(
        hold_kernel,
        out_shape=(sds((NY, WIDTH, FEAT), BF), sds((NY, FEAT, TEACH), BF)),
        in_specs=[pl.BlockSpec(memory_space=pl.ANY)] * 2,
        out_specs=tuple(whole(2)),
        scratch_shapes=[pltpu.SemaphoreType.DMA((2,))],
        compiler_params=params(1),
    )(win, wout)

    win_spec = pl.BlockSpec((1, WIDTH, FEAT), lambda i: (i, 0, 0))
    wout_spec = pl.BlockSpec((1, FEAT, TEACH), lambda i: (i, 0, 0))
    slab = pl.BlockSpec((PY, FEAT), lambda i: (0, i))
    early, preact, partial = pl.pallas_call(
        proj1_kernel,
        grid=(NY,),
        out_shape=(sds((PY, EARLY), BF), sds((PY, NY * FEAT), F32), sds((PY, TEACH), BF)),
        in_specs=[fixed((NS, PY, FEAT)), win_spec, wout_spec],
        out_specs=(fixed((PY, EARLY)), slab, fixed((PY, TEACH))),
        scratch_shapes=[pltpu.VMEM((PY, TEACH), F32)],
        compiler_params=params(),
    )(pooled_in, win, wout)
    early_in = gather(early, "seq", Y_GROUPS)
    partials = gather(partial, "seq", Z_GROUPS)

    back, late = pl.pallas_call(
        proj2_kernel,
        grid=(NY,),
        out_shape=(sds((NS, PY, FEAT), BF), sds((PY, LATE), BF)),
        in_specs=[fixed((NZ, PY, TEACH)), fixed((PY, TEACH)), slab, win_spec, wout_spec],
        out_specs=(fixed((NS, PY, FEAT)), fixed((PY, LATE))),
        scratch_shapes=[pltpu.VMEM((PY, WIDTH), F32)],
        compiler_params=params(),
    )(partials, targets, preact, win, wout)
    back_in = exchange(back, "seq")
    late_in = gather(late, "seq", Y_GROUPS)

    terms = pl.pallas_call(
        weights_kernel,
        out_shape=sds((WIDTH + TEACH, FEAT), BF),
        in_specs=whole(2),
        out_specs=whole(1)[0],
        compiler_params=params(),
    )(early_in, late_in)
    terms, back_in = lax.optimization_barrier((terms, back_in))
    part = exchange(terms.reshape(8, ROWS_DP, FEAT), "dp", XC_GROUPS)

    grad_rows, *moved = pl.pallas_call(
        value_grad_kernel,
        out_shape=(sds((PATCHES, FEAT), BF),) + (sds((NY, TOK, FEAT), BF),) * NZ,
        in_specs=whole(2),
        out_specs=tuple(whole(1 + NZ)),
        compiler_params=params(),
    )(back_in, pooled_probs)
    moved = [moved[0]] + [lax.ppermute(moved[k], "seq", Z_SHIFT[k]) for k in range(1, NZ)]
    grads = pl.pallas_call(
        bwd_kernel,
        grid=(LEN // BBLK,),
        out_shape=sds((NS, TOK, FEAT), BF),
        in_specs=[
            fixed((PATCHES, FEAT)),
            fixed((NS, ROWS, FEAT)),
            fixed((NS, TOK, FEAT)),
            pl.BlockSpec((2, BBLK, LEN), lambda i: (0, i, 0)),
        ],
        out_specs=pl.BlockSpec((BBLK // TOK, TOK, FEAT), lambda i: (i, 0, 0)),
        scratch_shapes=[
            pltpu.VMEM((BBLK, LEN), F32),
            pltpu.VMEM((BBLK, LEN), F32),
            pltpu.VMEM((BBLK, LEN), BF),
            pltpu.VMEM((BBLK, LEN), BF),
        ],
        compiler_params=params(50),
        cost_estimate=pl.CostEstimate(flops=10 ** 10, bytes_accessed=2 * 10 ** 7, transcendentals=0),
    )(grad_rows, x, values, probs)
    stacked = pl.pallas_call(
        stack_grad_kernel,
        out_shape=sds((NZ, NY, TOK, FEAT), BF),
        in_specs=whole(NZ),
        out_specs=whole(1)[0],
        compiler_params=params(),
    )(*moved)
    part, grads, stacked = lax.optimization_barrier((part, grads, stacked))
    part = pl.pallas_call(
        sum_kernel,
        out_shape=sds((ROWS_DP, FEAT), BF),
        in_specs=whole(1),
        out_specs=whole(1)[0],
        compiler_params=params(),
    )(part)
    part = gather(part, "dp", ZL_GROUPS)
    part, grads = lax.optimization_barrier((part, grads))
    grads_in = exchange(grads, "seq")
    part = pl.pallas_call(
        sum_kernel,
        out_shape=sds((ROWS_DP, FEAT), BF),
        in_specs=whole(1),
        out_specs=whole(1)[0],
        compiler_params=params(),
    )(part)
    total = gather(part, "dp", XC_GROUPS).reshape(WIDTH + TEACH, FEAT)
    grad_in, grad_out = pl.pallas_call(
        finish_kernel,
        out_shape=(sds((WIDTH, FEAT), F32), sds((FEAT, TEACH), F32)),
        in_specs=whole(1),
        out_specs=tuple(whole(2)),
        compiler_params=params(),
    )(total)

    grad_value = pl.pallas_call(
        join_grad_kernel,
        out_shape=sds((1, TOK, WIDTH), BF),
        in_specs=[pl.BlockSpec(memory_space=pl.ANY)],
        out_specs=whole(1)[0],
        scratch_shapes=[pltpu.VMEM((NS, TOK, FEAT), BF), pltpu.SemaphoreType.DMA((NS,))],
        compiler_params=params(59),
    )(gather(stacked, "seq", Y_GROUPS))
    grads_in, grad_value = lax.optimization_barrier((grads_in, grad_value))
    grad_query = pl.pallas_call(
        unpack_kernel,
        grid=(PARTS,),
        out_shape=sds((1, TOK, WIDTH), BF),
        in_specs=[chunk(TOK)],
        out_specs=columns,
        compiler_params=params(),
    )(grads_in)
    return (grad_query, grad_value, grad_in, grad_out)


def solution(mesh):
    placed = (
        P("dp", "seq", None),
        P("dp", "seq", None),
        P("dp", "seq", None),
        P("dp", "seq"),
        P("dp", "seq", None),
        P(None, "seq"),
        P("seq", None),
    )
    return jax.shard_map(
        per_device,
        mesh=mesh,
        in_specs=placed,
        out_specs=(P("dp", "seq", None), P("dp", "seq", None), P(None, "seq"), P("seq", None)),
        check_vma=False,
    )
```

```python
import functools

import jax
import jax.numpy as jnp
from jax import lax
from jax.experimental import pallas as pl
from jax.experimental.pallas import tpu as pltpu
from jax.sharding import PartitionSpec as P

BF = jnp.bfloat16
F32 = jnp.float32
NS = 16
NY = 4
NZ = 4
TOK = 128
LEN = 2048
FEAT = 128
PATCHES = 128
PY = 32
TEACH = 1408
WIDTH = 2048
GROUP = 16
EPSILON = 1e-06
ROWS = 2 * TOK + 16
TROWS = 96
EARLY = 4224
LATE = 1408 + 512
ROWS_DP = (2048 + 1408) // 8
FBLK = 512
BBLK = 256
CHUNK = 16
PARTS = 2
MIB = 1024 * 1024

Y_GROUPS = [[y * 4 + z for y in range(4)] for z in range(4)]
Z_GROUPS = [[y * 4 + z for z in range(4)] for y in range(4)]
Y_SHIFT = [[(y * 4 + z, (y + k) % 4 * 4 + z) for y in range(4) for z in range(4)] for k in range(4)]
Z_SHIFT = [[(y * 4 + z, y * 4 + (z + k) % 4) for y in range(4) for z in range(4)] for k in range(4)]
XC_GROUPS = [[x * 8 + zl * 2 + c for x in range(4) for c in range(2)] for zl in range(4)]
ZL_GROUPS = [[x * 8 + zl * 2 + c for zl in range(4)] for x in range(4) for c in range(2)]

NN = (((1,), (0,)), ((), ()))
NT = (((1,), (1,)), ((), ()))
TN = (((0,), (0,)), ((), ()))


def mm(a, b, dims=NN):
    return lax.dot_general(a, b, dims, preferred_element_type=F32)


def whole(n):
    return [pl.BlockSpec(memory_space=pltpu.VMEM)] * n


def params(mib=12):
    return pltpu.CompilerParams(vmem_limit_bytes=mib * MIB)


def sds(shape, dtype):
    return jax.ShapeDtypeStruct(shape, dtype)


def low_half(shape):
    return lax.broadcasted_iota(jnp.int32, shape, 1) < FEAT // 2


def of_head(array, head):
    keep = low_half(array.shape)
    zero = jnp.zeros_like(array)
    return jnp.where(keep, array, zero) if head == 0 else jnp.where(keep, zero, array)


def pack_kernel(q_ref, k_ref, ids_ref, out_ref):
    ids = jnp.broadcast_to(ids_ref[...].astype(F32), (16, TOK)).astype(BF)
    for i in range(NS // PARTS):
        cols = slice(i * FEAT, (i + 1) * FEAT)
        out_ref[i, 0:TOK, :] = q_ref[0, :, cols]
        out_ref[i, TOK:2 * TOK, :] = k_ref[0, :, cols]
        out_ref[i, 2 * TOK:ROWS, :] = ids


def split_value_kernel(v_ref, *out_refs):
    y = lax.axis_index("seq") // NZ
    for k in range(NY):
        for z in range(NZ):
            at = pl.multiple_of((y + k) % NY * (NZ * FEAT) + z * FEAT, FEAT)
            out_refs[k][z] = v_ref[0, :, pl.ds(at, FEAT)]


def turn_value_kernel(a_ref, b_ref, c_ref, d_ref, teacher_ref, *out_refs):
    z = lax.axis_index("seq") % NZ
    own = teacher_ref[0].astype(F32)
    for k in range(NZ):
        for c in range(0, TROWS // 8, 2):
            first = own[:, c * FEAT:(c + 1) * FEAT]
            second = own[:, (c + 1) * FEAT:(c + 2) * FEAT] if (c + 1) * FEAT < TEACH else first
            out_refs[k][c * 8:c * 8 + 16, :] = jnp.concatenate([first, second], axis=0).astype(BF)
        for i, ref in enumerate((a_ref, b_ref, c_ref, d_ref)):
            rows = slice(TROWS + i * TOK, TROWS + (i + 1) * TOK)
            out_refs[k][rows, :] = ref[(z + k) % NZ]


def selector(x_ref, first, count):
    parts = []
    for i in range(count):
        ids = x_ref[first + i, 2 * TOK:ROWS, :].astype(F32)[0:1, :]
        rows = lax.broadcasted_iota(jnp.int32, (PATCHES, TOK), 0).astype(F32)
        parts.append(jnp.where(rows == ids, 1.0, 0.0).astype(BF))
    return jnp.concatenate(parts, axis=1)


def fwd_kernel(x_ref, p_ref, pp_ref, acc_ref, s0_ref, s1_ref):
    block = pl.program_id(0)
    step = FBLK // TOK

    @pl.when(block == 0)
    def _():
        acc_ref[...] = jnp.zeros_like(acc_ref)

    keys = x_ref[:, TOK:2 * TOK, :].reshape(LEN, FEAT)
    queries = x_ref[pl.ds(block * step, step), 0:TOK, :].reshape(FBLK, FEAT)
    queries = (queries.astype(F32) * 0.125).astype(BF)
    sel = selector(x_ref, block * step, step)
    score_refs = (s0_ref, s1_ref)
    for head in range(2):
        score_refs[head][...] = mm(of_head(queries, head), keys, NT)
    for head in range(2):
        for c in range(0, FBLK, CHUNK):
            scores = score_refs[head][c:c + CHUNK, :]
            weights = jnp.exp(scores - jnp.max(scores, axis=1, keepdims=True))
            total = jnp.sum(weights, axis=1, keepdims=True)
            p_ref[head, c:c + CHUNK, :] = (weights * (1.0 / total)).astype(BF)
        acc_ref[head] += mm(sel, p_ref[head])

    @pl.when(block == pl.num_programs(0) - 1)
    def _():
        for head in range(2):
            pp_ref[head] = acc_ref[head].astype(BF)


def pool_kernel(pp_ref, a_ref, b_ref, c_ref, d_ref, send_ref, v_ref, target_ref):
    y = lax.axis_index("seq") // NZ
    z = lax.axis_index("seq") % NZ
    for k, ref in enumerate((a_ref, b_ref, c_ref, d_ref)):
        source = (z + NZ - k) % NZ
        for i in range(NY):
            v_ref[(y + NY - i) % NY * NZ + source] = ref[TROWS + i * TOK:TROWS + (i + 1) * TOK, :]
        at = pl.ds(pl.multiple_of(source * 8, 8), 8)
        for c in range(0, TROWS // 8, 2):
            pair = ref[c * 8:c * 8 + 16, :].astype(F32)
            target_ref[at, c * FEAT:(c + 1) * FEAT] = pair[0:8, :]
            if (c + 1) * FEAT < TEACH:
                target_ref[at, (c + 1) * FEAT:(c + 2) * FEAT] = pair[8:16, :]
    values = v_ref[...].reshape(LEN, FEAT)
    pooled = [mm(pp_ref[head], values) for head in range(2)]
    joined = jnp.where(low_half((PATCHES, FEAT)), pooled[0], pooled[1])
    joined = (joined * (1.0 / GROUP)).astype(BF)
    for d in range(NS):
        send_ref[d] = joined[d // NZ * PY:(d // NZ + 1) * PY, :]


def hold_kernel(a_ref, b_ref, a_out, b_out, sems):
    first = pltpu.make_async_copy(a_ref, a_out, sems.at[0])
    second = pltpu.make_async_copy(b_ref, b_out, sems.at[1])
    first.start()
    second.start()
    first.wait()
    second.wait()


def proj1_kernel(r_ref, win_ref, wout_ref, early_ref, preact_ref, send_ref, acc_ref):
    y = pl.program_id(0)

    @pl.when(y == 0)
    def _():
        for s in range(NS):
            early_ref[:, s * FEAT:(s + 1) * FEAT] = r_ref[s]
        early_ref[:, WIDTH + NY * FEAT:EARLY] = jnp.zeros((PY, EARLY - WIDTH - NY * FEAT), BF)
        acc_ref[...] = jnp.zeros_like(acc_ref)

    preact = mm(early_ref[:, 0:WIDTH], win_ref[0])
    hidden = (preact * jax.nn.sigmoid(preact)).astype(BF)
    preact_ref[...] = preact
    early_ref[:, pl.ds(pl.multiple_of(WIDTH + y * FEAT, FEAT), FEAT)] = hidden
    acc_ref[...] += mm(hidden, wout_ref[0])

    @pl.when(y == NY - 1)
    def _():
        send_ref[...] = acc_ref[...].astype(BF)


def proj2_kernel(
    r_ref, target_ref, preact_ref, win_ref, wout_ref, back_ref, late_ref, terms_ref
):
    y = pl.program_id(0)

    @pl.when(y == 0)
    def _():
        proj = r_ref[0].astype(F32)
        for z in range(1, NZ):
            proj = proj + r_ref[z].astype(F32)
        target = target_ref[...]
        scale = 1.0 / TEACH
        cross = jnp.sum(proj * target, axis=1, keepdims=True) * scale
        proj_power = jnp.sum(proj * proj, axis=1, keepdims=True) * scale + EPSILON
        teach_power = jnp.sum(target * target, axis=1, keepdims=True) * scale + EPSILON
        grad = -(target - cross / proj_power * proj) / jnp.sqrt(proj_power * teach_power)
        late_ref[:, 0:TEACH] = grad.astype(BF)
        terms_ref[...] = jnp.zeros_like(terms_ref)

    grad_hidden = mm(late_ref[:, 0:TEACH], wout_ref[0], NT)
    preact = preact_ref[...]
    sigma = jax.nn.sigmoid(preact)
    grad_pre = (grad_hidden * sigma * (1.0 + preact * (1.0 - sigma))).astype(BF)
    terms_ref[...] += mm(grad_pre, win_ref[0], NT)
    late_ref[:, pl.ds(pl.multiple_of(TEACH + y * FEAT, FEAT), FEAT)] = grad_pre

    @pl.when(y == NY - 1)
    def _():
        terms = terms_ref[...].astype(BF)
        for d in range(NS):
            back_ref[d] = terms[:, d * FEAT:(d + 1) * FEAT]


def value_grad_kernel(r_ref, pp_ref, g_ref, *out_refs):
    z = lax.axis_index("seq") % NZ
    for y in range(NY):
        summed = r_ref[y * NZ].astype(F32)
        for k in range(1, NZ):
            summed = summed + r_ref[y * NZ + k].astype(F32)
        rounded = summed.astype(BF).astype(F32) * (1.0 / GROUP)
        g_ref[y * PY:(y + 1) * PY, :] = rounded.astype(BF)
    grad = g_ref[...]
    for k in range(NZ):
        for y in range(NY):
            at = pl.multiple_of((y * NZ + (z + k) % NZ) * TOK, TOK)
            parts = [mm(pp_ref[head, :, pl.ds(at, TOK)], grad, TN) for head in range(2)]
            out_refs[k][y] = jnp.where(low_half((TOK, FEAT)), parts[0], parts[1]).astype(BF)


def stack_grad_kernel(a_ref, b_ref, c_ref, d_ref, out_ref):
    for k, ref in enumerate((a_ref, b_ref, c_ref, d_ref)):
        out_ref[k] = ref[...]


def join_grad_kernel(r_ref, out_ref, held_ref, sems):
    y = lax.axis_index("seq") // NZ
    z = lax.axis_index("seq") % NZ
    copies = []
    for source in range(NY):
        for k in range(NZ):
            n = source * NZ + k
            copies.append(pltpu.make_async_copy(r_ref.at[source, k, y], held_ref.at[n], sems.at[n]))
            copies[-1].start()
    for copy in copies:
        copy.wait()
    for source in range(NY):
        for k in range(NZ):
            at = pl.multiple_of((source * NZ + (z + NZ - k) % NZ) * FEAT, FEAT)
            out_ref[0, :, pl.ds(at, FEAT)] = held_ref[source * NZ + k]


def bwd_kernel(g_ref, x_ref, v_ref, p_ref, out_ref, d0_ref, d1_ref, w0_ref, w1_ref):
    block = pl.program_id(0)
    step = BBLK // TOK
    keys = x_ref[:, TOK:2 * TOK, :].reshape(LEN, FEAT)
    values = v_ref[...].reshape(LEN, FEAT)
    sel = selector(x_ref, block * step, step)
    upstream = (mm(sel, g_ref[...], TN) * 0.125).astype(BF)
    dprob_refs, work_refs = (d0_ref, d1_ref), (w0_ref, w1_ref)
    for head in range(2):
        dprob_refs[head][...] = mm(of_head(upstream, head), values, NT)
    parts = []
    for head in range(2):
        for c in range(0, BBLK, CHUNK):
            probs = p_ref[head, c:c + CHUNK, :].astype(F32)
            dprob = dprob_refs[head][c:c + CHUNK, :]
            delta = jnp.sum(probs * dprob, axis=1, keepdims=True)
            work_refs[head][c:c + CHUNK, :] = (probs * (dprob - delta)).astype(BF)
        parts.append(mm(work_refs[head][...], keys))
    rows = jnp.where(low_half((BBLK, FEAT)), parts[0], parts[1]).astype(BF)
    out_ref[...] = rows.reshape(step, TOK, FEAT)


def weights_kernel(early_ref, late_ref, out_ref):
    y = lax.axis_index("seq") // NZ
    at = pl.multiple_of(WIDTH + y * FEAT, FEAT)
    hidden = early_ref[:, :, pl.ds(at, FEAT)].reshape(PATCHES, FEAT)
    at = pl.multiple_of(TEACH + y * FEAT, FEAT)
    grad_pre = late_ref[:, :, pl.ds(at, FEAT)].reshape(PATCHES, FEAT)
    pooled = early_ref[:, :, 0:WIDTH].reshape(PATCHES, WIDTH)
    grad = late_ref[:, :, 0:TEACH].reshape(PATCHES, TEACH)
    out_ref[0:WIDTH, :] = mm(pooled, grad_pre, TN).astype(BF)
    grad_out = mm(hidden, grad, TN).astype(BF)
    for c in range(TEACH // FEAT):
        out_ref[WIDTH + c * FEAT:WIDTH + (c + 1) * FEAT, :] = grad_out[:, c * FEAT:(c + 1) * FEAT]


def sum_kernel(r_ref, out_ref):
    total = r_ref[0].astype(F32)
    for k in range(1, r_ref.shape[0]):
        total = total + r_ref[k].astype(F32)
    out_ref[...] = total.astype(BF)


def finish_kernel(r_ref, in_ref, out_ref):
    in_ref[...] = r_ref[0:WIDTH, :].astype(F32)
    for c in range(TEACH // FEAT):
        block = r_ref[WIDTH + c * FEAT:WIDTH + (c + 1) * FEAT, :]
        out_ref[:, c * FEAT:(c + 1) * FEAT] = block.astype(F32)


def unpack_kernel(r_ref, dq_ref):
    for i in range(NS // PARTS):
        dq_ref[0, :, i * FEAT:(i + 1) * FEAT] = r_ref[i]


def exchange(array, axis, groups=None):
    return lax.all_to_all(array, axis, 0, 0, axis_index_groups=groups, tiled=True)


def gather(array, axis, groups=None):
    return lax.all_gather(array, axis, axis=0, axis_index_groups=groups, tiled=False)


def fixed(shape):
    return pl.BlockSpec(shape, lambda i: (0,) * len(shape))


def per_device(query, key, value, patch_map, teacher, proj_in, proj_out):
    win = gather(proj_in, "seq", Y_GROUPS)
    wout = gather(proj_out, "seq", Y_GROUPS)
    columns = pl.BlockSpec((1, TOK, WIDTH // PARTS), lambda i: (0, 0, i))
    chunk = lambda rows: pl.BlockSpec((NS // PARTS, rows, FEAT), lambda i: (i, 0, 0))

    packed = pl.pallas_call(
        pack_kernel,
        grid=(PARTS,),
        out_shape=sds((NS, ROWS, FEAT), BF),
        in_specs=[columns, columns, fixed((1, TOK))],
        out_specs=chunk(ROWS),
        compiler_params=params(59),
    )(query, key, patch_map)
    packed, value, teacher = lax.optimization_barrier((packed, value, teacher))
    x = exchange(packed, "seq")
    pieces = pl.pallas_call(
        split_value_kernel,
        out_shape=(sds((NZ, TOK, FEAT), BF),) * NY,
        in_specs=whole(1),
        out_specs=tuple(whole(NY)),
        compiler_params=params(),
    )(value)
    pieces = [pieces[0]] + [lax.ppermute(pieces[k], "seq", Y_SHIFT[k]) for k in range(1, NY)]
    turned = pl.pallas_call(
        turn_value_kernel,
        out_shape=(sds((TROWS + NY * TOK, FEAT), BF),) * NZ,
        in_specs=whole(5),
        out_specs=tuple(whole(NZ)),
        compiler_params=params(),
    )(*pieces, teacher)
    turned = [turned[0]] + [lax.ppermute(turned[k], "seq", Z_SHIFT[k]) for k in range(1, NZ)]

    probs, pooled_probs = pl.pallas_call(
        fwd_kernel,
        grid=(LEN // FBLK,),
        out_shape=(sds((2, LEN, LEN), BF), sds((2, PATCHES, LEN), BF)),
        in_specs=[fixed((NS, ROWS, FEAT))],
        out_specs=(
            pl.BlockSpec((2, FBLK, LEN), lambda i: (0, i, 0)),
            fixed((2, PATCHES, LEN)),
        ),
        scratch_shapes=[
            pltpu.VMEM((2, PATCHES, LEN), F32),
            pltpu.VMEM((FBLK, LEN), F32),
            pltpu.VMEM((FBLK, LEN), F32),
        ],
        compiler_params=params(40),
        cost_estimate=pl.CostEstimate(flops=10 ** 6, bytes_accessed=10 ** 6, transcendentals=0),
    )(x)
    pooled_out, values, targets = pl.pallas_call(
        pool_kernel,
        out_shape=(sds((NS, PY, FEAT), BF), sds((NS, TOK, FEAT), BF), sds((PY, TEACH), F32)),
        in_specs=whole(5),
        out_specs=tuple(whole(3)),
        compiler_params=params(),
    )(pooled_probs, *turned)
    win, wout, pooled_out = lax.optimization_barrier((win, wout, pooled_out))
    pooled_in = exchange(pooled_out, "seq")
    win, wout = pl.pallas_call(
        hold_kernel,
        out_shape=(sds((NY, WIDTH, FEAT), BF), sds((NY, FEAT, TEACH), BF)),
        in_specs=[pl.BlockSpec(memory_space=pl.ANY)] * 2,
        out_specs=tuple(whole(2)),
        scratch_shapes=[pltpu.SemaphoreType.DMA((2,))],
        compiler_params=params(1),
    )(win, wout)

    win_spec = pl.BlockSpec((1, WIDTH, FEAT), lambda i: (i, 0, 0))
    wout_spec = pl.BlockSpec((1, FEAT, TEACH), lambda i: (i, 0, 0))
    slab = pl.BlockSpec((PY, FEAT), lambda i: (0, i))
    early, preact, partial = pl.pallas_call(
        proj1_kernel,
        grid=(NY,),
        out_shape=(sds((PY, EARLY), BF), sds((PY, NY * FEAT), F32), sds((PY, TEACH), BF)),
        in_specs=[fixed((NS, PY, FEAT)), win_spec, wout_spec],
        out_specs=(fixed((PY, EARLY)), slab, fixed((PY, TEACH))),
        scratch_shapes=[pltpu.VMEM((PY, TEACH), F32)],
        compiler_params=params(),
    )(pooled_in, win, wout)
    early_in = gather(early, "seq", Y_GROUPS)
    partials = gather(partial, "seq", Z_GROUPS)

    back, late = pl.pallas_call(
        proj2_kernel,
        grid=(NY,),
        out_shape=(sds((NS, PY, FEAT), BF), sds((PY, LATE), BF)),
        in_specs=[fixed((NZ, PY, TEACH)), fixed((PY, TEACH)), slab, win_spec, wout_spec],
        out_specs=(fixed((NS, PY, FEAT)), fixed((PY, LATE))),
        scratch_shapes=[pltpu.VMEM((PY, WIDTH), F32)],
        compiler_params=params(),
    )(partials, targets, preact, win, wout)
    back_in = exchange(back, "seq")
    late_in = gather(late, "seq", Y_GROUPS)

    terms = pl.pallas_call(
        weights_kernel,
        out_shape=sds((WIDTH + TEACH, FEAT), BF),
        in_specs=whole(2),
        out_specs=whole(1)[0],
        compiler_params=params(),
    )(early_in, late_in)
    terms, back_in = lax.optimization_barrier((terms, back_in))
    part = exchange(terms.reshape(8, ROWS_DP, FEAT), "dp", XC_GROUPS)

    grad_rows, *moved = pl.pallas_call(
        value_grad_kernel,
        out_shape=(sds((PATCHES, FEAT), BF),) + (sds((NY, TOK, FEAT), BF),) * NZ,
        in_specs=whole(2),
        out_specs=tuple(whole(1 + NZ)),
        compiler_params=params(),
    )(back_in, pooled_probs)
    moved = [moved[0]] + [lax.ppermute(moved[k], "seq", Z_SHIFT[k]) for k in range(1, NZ)]
    grads = pl.pallas_call(
        bwd_kernel,
        grid=(LEN // BBLK,),
        out_shape=sds((NS, TOK, FEAT), BF),
        in_specs=[
            fixed((PATCHES, FEAT)),
            fixed((NS, ROWS, FEAT)),
            fixed((NS, TOK, FEAT)),
            pl.BlockSpec((2, BBLK, LEN), lambda i: (0, i, 0)),
        ],
        out_specs=pl.BlockSpec((BBLK // TOK, TOK, FEAT), lambda i: (i, 0, 0)),
        scratch_shapes=[
            pltpu.VMEM((BBLK, LEN), F32),
            pltpu.VMEM((BBLK, LEN), F32),
            pltpu.VMEM((BBLK, LEN), BF),
            pltpu.VMEM((BBLK, LEN), BF),
        ],
        compiler_params=params(50),
        cost_estimate=pl.CostEstimate(flops=10 ** 10, bytes_accessed=2 * 10 ** 7, transcendentals=0),
    )(grad_rows, x, values, probs)
    stacked = pl.pallas_call(
        stack_grad_kernel,
        out_shape=sds((NZ, NY, TOK, FEAT), BF),
        in_specs=whole(NZ),
        out_specs=whole(1)[0],
        compiler_params=params(),
    )(*moved)
    part, grads, stacked = lax.optimization_barrier((part, grads, stacked))
    part = pl.pallas_call(
        sum_kernel,
        out_shape=sds((ROWS_DP, FEAT), BF),
        in_specs=whole(1),
        out_specs=whole(1)[0],
        compiler_params=params(),
    )(part)
    part = gather(part, "dp", ZL_GROUPS)
    part, grads = lax.optimization_barrier((part, grads))
    grads_in = exchange(grads, "seq")
    part = pl.pallas_call(
        sum_kernel,
        out_shape=sds((ROWS_DP, FEAT), BF),
        in_specs=whole(1),
        out_specs=whole(1)[0],
        compiler_params=params(),
    )(part)
    total = gather(part, "dp", XC_GROUPS).reshape(WIDTH + TEACH, FEAT)
    grad_in, grad_out = pl.pallas_call(
        finish_kernel,
        out_shape=(sds((WIDTH, FEAT), F32), sds((FEAT, TEACH), F32)),
        in_specs=whole(1),
        out_specs=tuple(whole(2)),
        compiler_params=params(),
    )(total)

    grad_value = pl.pallas_call(
        join_grad_kernel,
        out_shape=sds((1, TOK, WIDTH), BF),
        in_specs=[pl.BlockSpec(memory_space=pl.ANY)],
        out_specs=whole(1)[0],
        scratch_shapes=[pltpu.VMEM((NS, TOK, FEAT), BF), pltpu.SemaphoreType.DMA((NS,))],
        compiler_params=params(59),
    )(gather(stacked, "seq", Y_GROUPS))
    grads_in, grad_value = lax.optimization_barrier((grads_in, grad_value))
    grad_query = pl.pallas_call(
        unpack_kernel,
        grid=(PARTS,),
        out_shape=sds((1, TOK, WIDTH), BF),
        in_specs=[chunk(TOK)],
        out_specs=columns,
        compiler_params=params(),
    )(grads_in)
    return (grad_query, grad_value, grad_in, grad_out)


def solution(mesh):
    placed = (
        P("dp", "seq", None),
        P("dp", "seq", None),
        P("dp", "seq", None),
        P("dp", "seq"),
        P("dp", "seq", None),
        P(None, "seq"),
        P("seq", None),
    )
    return jax.shard_map(
        per_device,
        mesh=mesh,
        in_specs=placed,
        out_specs=(P("dp", "seq", None), P("dp", "seq", None), P(None, "seq"), P("seq", None)),
        check_vma=False,
    )
```
